512 devices in a mesh: dp: 32 (over z, y_lo, core), tensor: 16 (over y_hi, x).
Axes of the slice: x: 4, y: 8 (y_hi: 4, y_lo: 2; y = y_hi * 2 + y_lo), z: 8, core: 2. Of those that a mesh axis runs over, the one named last changes fastest.
Arguments:
- activations: bfloat16 [512, 8192], P('tensor', 'dp'), may hold values from -6 to 6
- gate_weight: bfloat16 [8192, 28672], P('dp', 'tensor'), may hold values from -0.0625 to 0.0625
- up_weight: bfloat16 [8192, 28672], P('dp', 'tensor'), may hold values from -0.0625 to 0.0625
- hidden_grad: bfloat16 [512, 28672], P('dp', 'tensor'), may hold values from -1.5 to 1.5
Outputs:
- hidden: bfloat16 [512, 28672], P('dp', 'tensor')
- input_grad: bfloat16 [512, 8192], P('tensor', 'dp')
- gate_grad: bfloat16 [8192, 28672], P('dp', 'tensor')
- up_grad: bfloat16 [8192, 28672], P('dp', 'tensor')
The draws below stay inside these ranges and needn't reach their ends.
All inputs are finite; a program needn't handle non-finite values.
Results may differ from the reference program's by a relative error of at most 0.0049.
Values may be sent and summed in bfloat16 or wider, within the bound.
No kernel may reach another device: no remote copies, remote signals or barrier semaphores. Data moves between devices by JAX's collectives and lax.ppermute only.
A program may use at most 64 MiB of HBM per device.

```python
import jax
import jax.numpy as jnp

D = 8192
FF = 28672
TOKENS = 512


def block_scale(stream_key, extent, split, least, high):
    level, own = 1.0, jax.random.fold_in(stream_key, 6)
    for position, shards_of in split:
        heights = jnp.exp(jax.random.uniform(jax.random.fold_in(own, position), (shards_of,), jnp.float32, least / len(split), high / len(split)))
        level = level * jnp.repeat(heights, extent[position] // shards_of).reshape([-1 if axis == position else 1 for axis in range(len(extent))])
    return level


def noise(rng, shape, scale, reach, split=(), held_as=jnp.bfloat16):
    factor_of = block_scale(rng, shape, split, -0.22, 0.18) if split else 1.0
    result = jax.random.normal(rng, shape, jnp.float32) * scale * factor_of
    return jnp.minimum(jnp.maximum(result, -reach), reach).astype(held_as)


def setup_inputs(seed: int = 0) -> dict:
    seeds = jax.random.split(jax.random.key(seed), 5)
    return {
        "activations": noise(seeds[0], (TOKENS, D), 1.0, 6.0, ((0, 16), (1, 32))),
        "gate_weight": noise(seeds[1], (D, FF), D ** -0.5, 0.0625, ((0, 32), (1, 16))),
        "up_weight": noise(seeds[2], (D, FF), D ** -0.5, 0.0625, ((0, 32), (1, 16))),
        "hidden_grad": noise(seeds[3], (TOKENS, FF), 0.25, 1.5, ((0, 32), (1, 16))),
    }


def reference(activations, gate_weight, up_weight, hidden_grad):
    gate_pre = jnp.dot(activations, gate_weight, preferred_element_type=jnp.float32)
    up_pre = jnp.dot(activations, up_weight, preferred_element_type=jnp.float32)
    sigmoid_gate = jax.nn.sigmoid(gate_pre)
    hidden = (gate_pre * sigmoid_gate * up_pre).astype(jnp.bfloat16)
    cotangent = hidden_grad.astype(jnp.float32)
    gate_back = (cotangent * up_pre * sigmoid_gate * (1.0 + gate_pre * (1.0 - sigmoid_gate))).astype(jnp.bfloat16)
    up_back = (cotangent * gate_pre * sigmoid_gate).astype(jnp.bfloat16)
    input_grad = (jnp.dot(gate_back, gate_weight.T, preferred_element_type=jnp.float32)
                  + jnp.dot(up_back, up_weight.T, preferred_element_type=jnp.float32)).astype(jnp.bfloat16)
    gate_grad = jnp.dot(activations.T, gate_back, preferred_element_type=jnp.float32).astype(jnp.bfloat16)
    up_grad = jnp.dot(activations.T, up_back, preferred_element_type=jnp.float32).astype(jnp.bfloat16)
    return hidden, input_grad, gate_grad, up_grad
```

```python
import jax
import jax.numpy as jnp
from jax import lax
from jax.sharding import PartitionSpec as P

F32, BF16 = jnp.float32, jnp.bfloat16

Y_SWAP = [(i, i ^ 2) for i in range(32)]
CORE_SWAP = [(i, i ^ 1) for i in range(32)]
Z_GROUPS = [[z * 4 + r for z in range(8)] for r in range(4)]


def dot(a, b):
    return jnp.dot(a, b, preferred_element_type=F32)


def dot_nt(a, b):
    return lax.dot_general(a, b, (((1,), (1,)), ((), ())), preferred_element_type=F32)


def dot_tn(a, b):
    return lax.dot_general(a, b, (((0,), (0,)), ((), ())), preferred_element_type=F32)


def swap_y(x):
    return lax.ppermute(x, "dp", Y_SWAP)


def swap_core(x):
    return lax.ppermute(x, "dp", CORE_SWAP)


def ordered(first, mine, other, axis):
    return jnp.where(
        first,
        jnp.concatenate([mine, other], axis),
        jnp.concatenate([other, mine], axis),
    )


def per_device(activations, gate_weight, up_weight, hidden_grad):
    index = lax.axis_index("dp")
    y0 = (index // 2) % 2 == 0
    c0 = index % 2 == 0
    tensor = lax.axis_size("tensor")
    rows, width = activations.shape
    half = gate_weight.shape[1] // 2
    block = hidden_grad.shape[0]

    def pick(cond, a, b):
        return jnp.where(cond, a, b)

    lo = jnp.concatenate([gate_weight[:, :half], up_weight[:, :half]], 1)
    hi = jnp.concatenate([gate_weight[:, half:], up_weight[:, half:]], 1)
    weight_own = pick(y0, lo, hi)
    weight_peer = swap_y(pick(y0, hi, lo))

    tokens = lax.all_to_all(
        jnp.broadcast_to(activations[None], (tensor, rows, width)), "tensor", 0, 0
    )
    tokens = tokens.reshape(-1, 2, block, width)
    even = tokens[:, 0].reshape(-1, width)
    odd = tokens[:, 1].reshape(-1, width)
    keep_own, send_own = pick(c0, even, odd), pick(c0, odd, even)
    peer = swap_y(jnp.concatenate([keep_own, send_own], 0))
    count = keep_own.shape[0]
    keep_peer, send_peer = peer[:count], peer[count:]

    sent = (dot(send_own, weight_own) + dot(send_peer, weight_peer)).astype(BF16)
    got = swap_core(sent)
    kept = dot(keep_own, weight_own) + dot(keep_peer, weight_peer)
    part = (kept + got.astype(F32)).astype(BF16)
    part = part.reshape(8, 2 * block, 2 * half)
    part = lax.all_to_all(part, "dp", 0, 0, axis_index_groups=Z_GROUPS)
    pre = jnp.sum(part.astype(F32), 0)
    gate_pre, up_pre = pre[:, :half], pre[:, half:]

    grad_lo, grad_hi = hidden_grad[:, :half], hidden_grad[:, half:]
    grad = ordered(
        y0, pick(y0, grad_lo, grad_hi), swap_y(pick(y0, grad_hi, grad_lo)), 0
    ).astype(F32)

    sig = jax.nn.sigmoid(gate_pre)
    hidden = (gate_pre * sig * up_pre).astype(BF16)
    gate_back = (grad * up_pre * sig * (1.0 + gate_pre * (1.0 - sig))).astype(BF16)
    up_back = (grad * gate_pre * sig).astype(BF16)
    back = jnp.concatenate([gate_back, up_back], 1)

    back_own = lax.all_gather(back, "dp", axis=0, tiled=True, axis_index_groups=Z_GROUPS)
    back_other = swap_core(back_own)

    h_lo, h_hi = hidden[:block], hidden[block:]
    hidden = ordered(y0, pick(y0, h_lo, h_hi), swap_y(pick(y0, h_hi, h_lo)), 1)

    def input_part(weight):
        own, other = dot_nt(back_own, weight), dot_nt(back_other, weight)
        shape = (-1, 1, block, width)
        return ordered(c0, own.reshape(shape), other.reshape(shape), 1)

    peer_part = swap_y(input_part(weight_peer).astype(BF16))
    total = (input_part(weight_own) + peer_part.astype(F32)).astype(BF16)
    total = lax.all_to_all(total.reshape(tensor, rows, width), "tensor", 0, 0)
    input_grad = jnp.sum(total.astype(F32), 0).astype(BF16)

    def weight_part(keep, send):
        return (dot_tn(keep, back_own) + dot_tn(send, back_other)).astype(BF16)

    from_peer = swap_y(weight_part(keep_peer, send_peer))
    mine = weight_part(keep_own, send_own)
    gate_grad = ordered(y0, mine[:, :half], from_peer[:, :half], 1)
    up_grad = ordered(y0, mine[:, half:], from_peer[:, half:], 1)
    return (hidden, input_grad, gate_grad, up_grad)


def solution(mesh):
    placed = (P("tensor", "dp"), P("dp", "tensor"), P("dp", "tensor"), P("dp", "tensor"))
    return jax.shard_map(
        per_device,
        mesh=mesh,
        in_specs=placed,
        out_specs=(P("dp", "tensor"), P("tensor", "dp"), P("dp", "tensor"), P("dp", "tensor")),
        check_vma=False,
    )
```

```python
import jax
import jax.numpy as jnp
from jax import lax
from jax.experimental import pallas as pl
from jax.experimental.pallas import tpu as pltpu
from jax.sharding import PartitionSpec as P

F32, BF16 = jnp.float32, jnp.bfloat16

CORE_SWAP = [(i, i ^ 1) for i in range(32)]
Y_SWAP = [(i, i ^ 2) for i in range(32)]
QUAD_SWAP = [None, Y_SWAP, [(i, i ^ 4) for i in range(32)], [(i, i ^ 6) for i in range(32)]]
Z_GROUPS = [[z * 4 + r for z in range(8)] for r in range(4)]
X_GROUPS = [[4 * h + x for x in range(4)] for h in range(4)]
QUAD_YHI_GROUPS = [
    [((2 * q + b) * 4 + 2 * y + c) * 16 + 4 * h + x for b in range(2) for y in range(2) for h in range(4)]
    for q in range(4) for c in range(2) for x in range(4)
]

PARAMS = pltpu.CompilerParams(vmem_limit_bytes=32 * 1024 * 1024)
VMEM = pl.BlockSpec(memory_space=pltpu.VMEM)
SMEM = pl.BlockSpec(memory_space=pltpu.SMEM)


def struct(shape, dtype=BF16):
    return jax.ShapeDtypeStruct(shape, dtype)


def call(kernel, n_in, out_shape, flops):
    many = isinstance(out_shape, list)
    return pl.pallas_call(
        kernel,
        out_shape=out_shape,
        in_specs=[SMEM] + [VMEM] * n_in,
        out_specs=[VMEM] * len(out_shape) if many else VMEM,
        compiler_params=PARAMS,
        cost_estimate=pl.CostEstimate(flops=flops, bytes_accessed=4 << 20, transcendentals=0),
    )


def spans(n, step=256):
    return [slice(i, min(i + step, n)) for i in range(0, n, step)]


def arrange_and_send(place, raw, w0, w1, w2, w3, tokens, sent):
    width = raw.shape[-1]
    half, block = tokens.shape[0] // 2, raw.shape[-2]
    for part in range(2):
        core = place[1] ^ part
        for k in range(4):
            member = place[0] ^ k
            for h in range(4):
                for x in range(4):
                    row = part * half + (h * 4 + x) * block
                    tokens[row : row + block, k * width : (k + 1) * width] = raw[x, member, h, core]
    for s in spans(sent.shape[1]):
        total = None
        for k, w in enumerate((w0, w1, w2, w3)):
            term = jnp.dot(
                tokens[half:, k * width : (k + 1) * width], w[:, s], preferred_element_type=F32
            )
            total = term if total is None else total + term
        sent[:, s] = total


def keep_sums(place, tokens, w0, w1, w2, w3, got, out):
    width = w0.shape[0]
    half = out.shape[0]
    for s in spans(out.shape[1]):
        total = got[:, s]
        for k, w in enumerate((w0, w1, w2, w3)):
            total = total + jnp.dot(
                tokens[:half, k * width : (k + 1) * width], w[:, s], preferred_element_type=F32
            )
        out[:, s] = total.astype(BF16)


def input_parts(place, own, other, w0, w1, w2, w3, out):
    block = out.shape[-2]
    for part, back in enumerate((own, other)):
        core = place[1] ^ part
        for k, w in enumerate((w0, w1, w2, w3)):
            member = place[0] ^ k
            term = lax.dot_general(
                back[...], w[...], (((1,), (1,)), ((), ())), preferred_element_type=F32
            ).astype(BF16)
            for h in range(4):
                for x in range(4):
                    row = (h * 4 + x) * block
                    out[x, member, h, core] = term[row : row + block]


def weight_parts(place, tokens, own, other, *outs):
    width, n = outs[0].shape
    half = own.shape[0]
    dims = (((0,), (0,)), ((), ()))
    for k, out in enumerate(outs):
        for s in spans(n):
            cols = slice(k * width, (k + 1) * width)
            term = lax.dot_general(tokens[:half, cols], own[:, s], dims, preferred_element_type=F32)
            term += lax.dot_general(tokens[half:, cols], other[:, s], dims, preferred_element_type=F32)
            out[:, s] = term.astype(BF16)


def after(x, *others):
    return lax.optimization_barrier((x, *others))[0]


def per_device(activations, gate_weight, up_weight, hidden_grad):
    index = lax.axis_index("dp")
    core, y, z_bit = index & 1, (index >> 1) & 1, (index >> 2) & 1
    y0, z0 = y == 0, z_bit == 0
    place = jnp.stack([z_bit * 2 + y, core]).astype(jnp.int32)
    rows, width = activations.shape
    half = gate_weight.shape[1] // 2
    block = hidden_grad.shape[0]
    count = 16 * block
    flops = 2 * count * 4 * width * half

    def pick(cond, a, b):
        return jnp.where(cond, a, b)

    def by_member(parts):
        a = [pick(y0, parts[i], parts[i ^ 1]) for i in range(4)]
        return [pick(z0, a[i], a[i ^ 2]) for i in range(4)]

    def pair(mine, other):
        return pick(y0, mine, other), pick(y0, other, mine)

    pieces = by_member(
        [gate_weight[:, :half], gate_weight[:, half:], up_weight[:, :half], up_weight[:, half:]]
    )
    weights = [pieces[0]] + [lax.ppermute(pieces[k], "dp", QUAD_SWAP[k]) for k in (1, 2, 3)]

    raw = lax.all_to_all(
        jnp.broadcast_to(activations[None], (16, rows, width)), ("dp", "tensor"), 0, 0,
        axis_index_groups=QUAD_YHI_GROUPS,
    )
    raw = after(raw, weights[1])
    raw = lax.all_to_all(
        jnp.broadcast_to(raw[None], (4, 16, rows, width)), "tensor", 0, 0, axis_index_groups=X_GROUPS
    )
    raw = raw.reshape(4, 4, 4, 2, block, width)

    tokens, sent = call(
        arrange_and_send, 5, [struct((2 * count, 4 * width)), struct((count, half), F32)], flops
    )(place, raw, *weights)
    got = lax.ppermute(sent, "dp", CORE_SWAP)
    part = call(keep_sums, 6, struct((count, half)), flops)(place, tokens, *weights, got)
    part = lax.all_to_all(part.reshape(8, 2 * block, half), "dp", 0, 0, axis_index_groups=Z_GROUPS)
    gate_pre = jnp.sum(part[0::2].astype(F32), 0)
    up_pre = jnp.sum(part[1::2].astype(F32), 0)

    lo, hi = hidden_grad[:, :half], hidden_grad[:, half:]
    mine, other = pair(lo, hi)
    grad = jnp.concatenate(pair(mine, lax.ppermute(other, "dp", Y_SWAP)), 0).astype(F32)

    sig = jax.nn.sigmoid(gate_pre)
    hidden = (gate_pre * sig * up_pre).astype(BF16)
    gate_back = (grad * up_pre * sig * (1.0 + gate_pre * (1.0 - sig))).astype(BF16)
    up_back = (grad * gate_pre * sig).astype(BF16)

    own = lax.all_to_all(
        jnp.stack([gate_back, up_back] * 4), "dp", 0, 0, axis_index_groups=Z_GROUPS
    ).reshape(count, half)
    mine, other = pair(hidden[:block], hidden[block:])
    other = lax.ppermute(other, "dp", Y_SWAP)
    own = after(own, other)
    hidden = jnp.concatenate(pair(mine, other), 1)
    other = lax.ppermute(own, "dp", CORE_SWAP)

    total = call(input_parts, 6, struct((4, 4, 4, 2, block, width)), 2 * flops)(
        place, own, other, *weights
    )
    total = lax.all_to_all(
        total.reshape(4, 16, rows, width), "tensor", 0, 0, axis_index_groups=X_GROUPS
    )
    total = jnp.sum(total.astype(F32), 0).astype(BF16)

    grads = call(weight_parts, 3, [struct((width, half))] * 4, 2 * flops)(place, tokens, own, other)
    grads = [grads[0]] + [lax.ppermute(grads[k], "dp", QUAD_SWAP[k]) for k in (1, 2, 3)]

    total = after(total, grads[1])
    total = lax.all_to_all(total, ("dp", "tensor"), 0, 0, axis_index_groups=QUAD_YHI_GROUPS)
    input_grad = jnp.sum(total.astype(F32), 0).astype(BF16)

    grads = by_member(grads)
    gate_grad = jnp.concatenate(grads[:2], 1)
    up_grad = jnp.concatenate(grads[2:], 1)
    return (hidden, input_grad, gate_grad, up_grad)


def solution(mesh):
    placed = (P("tensor", "dp"), P("dp", "tensor"), P("dp", "tensor"), P("dp", "tensor"))
    return jax.shard_map(
        per_device,
        mesh=mesh,
        in_specs=placed,
        out_specs=(P("dp", "tensor"), P("tensor", "dp"), P("dp", "tensor"), P("dp", "tensor")),
        check_vma=False,
    )
```

```python
import jax
import jax.numpy as jnp
from jax import lax
from jax.experimental import pallas as pl
from jax.experimental.pallas import tpu as pltpu
from jax.sharding import PartitionSpec as P

F32, BF16 = jnp.float32, jnp.bfloat16

CORE_SWAP = [(i, i ^ 1) for i in range(32)]
Y_SWAP = [(i, i ^ 2) for i in range(32)]
QUAD_SWAP = [None, Y_SWAP, [(i, i ^ 4) for i in range(32)], [(i, i ^ 6) for i in range(32)]]
Z_GROUPS = [[z * 4 + r for z in range(8)] for r in range(4)]
X_GROUPS = [[4 * h + x for x in range(4)] for h in range(4)]
QUAD_YHI_GROUPS = [
    [((2 * q + b) * 4 + 2 * y + c) * 16 + 4 * h + x for b in range(2) for y in range(2) for h in range(4)]
    for q in range(4) for c in range(2) for x in range(4)
]

PARAMS = pltpu.CompilerParams(vmem_limit_bytes=32 * 1024 * 1024)
VMEM = pl.BlockSpec(memory_space=pltpu.VMEM)
SMEM = pl.BlockSpec(memory_space=pltpu.SMEM)


def struct(shape, dtype=BF16):
    return jax.ShapeDtypeStruct(shape, dtype)


def call(kernel, n_in, out_shape, flops):
    many = isinstance(out_shape, list)
    return pl.pallas_call(
        kernel,
        out_shape=out_shape,
        in_specs=[SMEM] + [VMEM] * n_in,
        out_specs=[VMEM] * len(out_shape) if many else VMEM,
        compiler_params=PARAMS,
        cost_estimate=pl.CostEstimate(flops=flops, bytes_accessed=4 << 20, transcendentals=0),
    )


def spans(n, step=256):
    return [slice(i, min(i + step, n)) for i in range(0, n, step)]


def arrange_and_send(place, raw, w0, w1, w2, w3, tokens, sent):
    width = raw.shape[-1]
    half, block = tokens.shape[0] // 2, raw.shape[-2]
    for part in range(2):
        core = place[1] ^ part
        for k in range(4):
            member = place[0] ^ k
            for h in range(4):
                for x in range(4):
                    row = part * half + (h * 4 + x) * block
                    tokens[row : row + block, k * width : (k + 1) * width] = raw[x, member, h, core]
    for s in spans(sent.shape[1]):
        total = None
        for k, w in enumerate((w0, w1, w2, w3)):
            term = jnp.dot(
                tokens[half:, k * width : (k + 1) * width], w[:, s], preferred_element_type=F32
            )
            total = term if total is None else total + term
        sent[:, s] = total


def keep_sums(place, tokens, w0, w1, w2, w3, out):
    width = w0.shape[0]
    half = out.shape[0]
    for s in spans(out.shape[1]):
        total = None
        for k, w in enumerate((w0, w1, w2, w3)):
            term = jnp.dot(
                tokens[:half, k * width : (k + 1) * width], w[:, s], preferred_element_type=F32
            )
            total = term if total is None else total + term
        out[:, s] = total


def input_parts(place, own, other, w0, w1, w2, w3, out):
    block = out.shape[-2]
    for part, back in enumerate((own, other)):
        core = place[1] ^ part
        for k, w in enumerate((w0, w1, w2, w3)):
            member = place[0] ^ k
            term = lax.dot_general(
                back[...], w[...], (((1,), (1,)), ((), ())), preferred_element_type=F32
            ).astype(BF16)
            for h in range(4):
                for x in range(4):
                    row = (h * 4 + x) * block
                    out[x, member, h, core] = term[row : row + block]


def weight_parts(place, tokens, own, other, *outs):
    width, n = outs[0].shape
    half = own.shape[0]
    dims = (((0,), (0,)), ((), ()))
    for k, out in enumerate(outs):
        for s in spans(n):
            cols = slice(k * width, (k + 1) * width)
            term = lax.dot_general(tokens[:half, cols], own[:, s], dims, preferred_element_type=F32)
            term += lax.dot_general(tokens[half:, cols], other[:, s], dims, preferred_element_type=F32)
            out[:, s] = term.astype(BF16)


def after(x, *others):
    return lax.optimization_barrier((x, *others))[0]


def per_device(activations, gate_weight, up_weight, hidden_grad):
    index = lax.axis_index("dp")
    core, y, z_bit = index & 1, (index >> 1) & 1, (index >> 2) & 1
    y0, z0 = y == 0, z_bit == 0
    place = jnp.stack([z_bit * 2 + y, core]).astype(jnp.int32)
    rows, width = activations.shape
    half = gate_weight.shape[1] // 2
    block = hidden_grad.shape[0]
    count = 16 * block
    flops = 2 * count * 4 * width * half

    def pick(cond, a, b):
        return jnp.where(cond, a, b)

    def by_member(parts):
        a = [pick(y0, parts[i], parts[i ^ 1]) for i in range(4)]
        return [pick(z0, a[i], a[i ^ 2]) for i in range(4)]

    def pair(mine, other):
        return pick(y0, mine, other), pick(y0, other, mine)

    pieces = by_member(
        [gate_weight[:, :half], gate_weight[:, half:], up_weight[:, :half], up_weight[:, half:]]
    )
    weights = [pieces[0]] + [lax.ppermute(pieces[k], "dp", QUAD_SWAP[k]) for k in (1, 2, 3)]

    raw = lax.all_to_all(
        jnp.broadcast_to(activations[None], (16, rows, width)), ("dp", "tensor"), 0, 0,
        axis_index_groups=QUAD_YHI_GROUPS,
    )
    raw = after(raw, weights[1], weights[2])
    raw = lax.all_to_all(
        jnp.broadcast_to(raw[None], (4, 16, rows, width)), "tensor", 0, 0, axis_index_groups=X_GROUPS
    )
    raw = raw.reshape(4, 4, 4, 2, block, width)

    tokens, sent = call(
        arrange_and_send, 5, [struct((2 * count, 4 * width)), struct((count, half), F32)], flops
    )(place, raw, *weights)
    got = lax.ppermute(sent, "dp", CORE_SWAP)
    kept = call(keep_sums, 5, struct((count, half), F32), flops)(place, tokens, *weights)
    part = (kept + got).astype(BF16)
    part = lax.all_to_all(part.reshape(8, 2 * block, half), "dp", 0, 0, axis_index_groups=Z_GROUPS)
    gate_pre = jnp.sum(part[0::2].astype(F32), 0)
    up_pre = jnp.sum(part[1::2].astype(F32), 0)

    lo, hi = hidden_grad[:, :half], hidden_grad[:, half:]
    mine, other = pair(lo, hi)
    grad = jnp.concatenate(pair(mine, lax.ppermute(other, "dp", Y_SWAP)), 0).astype(F32)

    sig = jax.nn.sigmoid(gate_pre)
    hidden = (gate_pre * sig * up_pre).astype(BF16)
    gate_back = (grad * up_pre * sig * (1.0 + gate_pre * (1.0 - sig))).astype(BF16)
    up_back = (grad * gate_pre * sig).astype(BF16)

    own = lax.all_to_all(
        jnp.broadcast_to(jnp.stack([gate_back, up_back])[None], (4, 2, 2 * block, half)).reshape(
            8, 2 * block, half
        ),
        "dp", 0, 0, axis_index_groups=Z_GROUPS,
    ).reshape(count, half)
    mine, other = pair(hidden[:block], hidden[block:])
    other = lax.ppermute(other, "dp", Y_SWAP)
    own = after(own, other)
    hidden = jnp.concatenate(pair(mine, other), 1)
    other = lax.ppermute(own, "dp", CORE_SWAP)

    total = call(input_parts, 6, struct((4, 4, 4, 2, block, width)), 2 * flops)(
        place, own, other, *weights
    )
    total = lax.all_to_all(
        total.reshape(4, 16, rows, width), "tensor", 0, 0, axis_index_groups=X_GROUPS
    )
    total = jnp.sum(total.astype(F32), 0).astype(BF16)

    grads = call(weight_parts, 3, [struct((width, half))] * 4, 2 * flops)(place, tokens, own, other)
    grads = [grads[0]] + [lax.ppermute(grads[k], "dp", QUAD_SWAP[k]) for k in (1, 2, 3)]

    total = after(total, grads[1])
    total = lax.all_to_all(total, ("dp", "tensor"), 0, 0, axis_index_groups=QUAD_YHI_GROUPS)
    input_grad = jnp.sum(total.astype(F32), 0).astype(BF16)

    grads = by_member(grads)
    gate_grad = jnp.concatenate(grads[:2], 1)
    up_grad = jnp.concatenate(grads[2:], 1)
    return (hidden, input_grad, gate_grad, up_grad)


def solution(mesh):
    placed = (P("tensor", "dp"), P("dp", "tensor"), P("dp", "tensor"), P("dp", "tensor"))
    return jax.shard_map(
        per_device,
        mesh=mesh,
        in_specs=placed,
        out_specs=(P("dp", "tensor"), P("tensor", "dp"), P("dp", "tensor"), P("dp", "tensor")),
        check_vma=False,
    )
```

```python
import jax
import jax.numpy as jnp
from jax import lax
from jax.experimental import pallas as pl
from jax.experimental.pallas import tpu as pltpu
from jax.sharding import PartitionSpec as P

F32, BF16 = jnp.float32, jnp.bfloat16

CORE_SWAP = [(i, i ^ 1) for i in range(32)]
Y_SWAP = [(i, i ^ 2) for i in range(32)]
QUAD_SWAP = [None, Y_SWAP, [(i, i ^ 4) for i in range(32)], [(i, i ^ 6) for i in range(32)]]
Z_GROUPS = [[z * 4 + r for z in range(8)] for r in range(4)]
X_GROUPS = [[4 * h + x for x in range(4)] for h in range(4)]
QUAD_YHI_GROUPS = [
    [((2 * q + b) * 4 + 2 * y + c) * 16 + 4 * h + x for b in range(2) for y in range(2) for h in range(4)]
    for q in range(4) for c in range(2) for x in range(4)
]

PARAMS = pltpu.CompilerParams(vmem_limit_bytes=32 * 1024 * 1024)
MARK_FLOPS = 30_000_000_000
VMEM = pl.BlockSpec(memory_space=pltpu.VMEM)
SMEM = pl.BlockSpec(memory_space=pltpu.SMEM)


def struct(shape, dtype=BF16):
    return jax.ShapeDtypeStruct(shape, dtype)


def call(kernel, n_in, out_shape, flops):
    many = isinstance(out_shape, list)
    return pl.pallas_call(
        kernel,
        out_shape=out_shape,
        in_specs=[SMEM] + [VMEM] * n_in,
        out_specs=[VMEM] * len(out_shape) if many else VMEM,
        compiler_params=PARAMS,
        cost_estimate=pl.CostEstimate(flops=flops, bytes_accessed=4 << 20, transcendentals=0),
    )


def spans(n, step=256):
    return [slice(i, min(i + step, n)) for i in range(0, n, step)]


def arrived(w1, w2, w3, out):
    out[...] = jnp.zeros_like(out)


def arrange_and_send(place, mark, raw, w0, w1, w2, w3, tokens, sent):
    width = raw.shape[-1]
    half, block = tokens.shape[0] // 2, raw.shape[-2]
    for part in range(2):
        core = place[1] ^ part
        for k in range(4):
            member = place[0] ^ k
            for h in range(4):
                for x in range(4):
                    row = part * half + (h * 4 + x) * block
                    tokens[row : row + block, k * width : (k + 1) * width] = raw[x, member, h, core]
    for s in spans(sent.shape[1]):
        total = None
        for k, w in enumerate((w0, w1, w2, w3)):
            term = jnp.dot(
                tokens[half:, k * width : (k + 1) * width], w[:, s], preferred_element_type=F32
            )
            total = term if total is None else total + term
        sent[:, s] = total


def keep_sums(place, tokens, w0, w1, w2, w3, out):
    width = w0.shape[0]
    half = out.shape[0]
    for s in spans(out.shape[1]):
        total = None
        for k, w in enumerate((w0, w1, w2, w3)):
            term = jnp.dot(
                tokens[:half, k * width : (k + 1) * width], w[:, s], preferred_element_type=F32
            )
            total = term if total is None else total + term
        out[:, s] = total


def input_parts(place, own, other, w0, w1, w2, w3, out):
    block = out.shape[-2]
    for part, back in enumerate((own, other)):
        core = place[1] ^ part
        for k, w in enumerate((w0, w1, w2, w3)):
            member = place[0] ^ k
            term = lax.dot_general(
                back[...], w[...], (((1,), (1,)), ((), ())), preferred_element_type=F32
            ).astype(BF16)
            for h in range(4):
                for x in range(4):
                    row = (h * 4 + x) * block
                    out[x, member, h, core] = term[row : row + block]


def weight_parts(place, tokens, own, other, *outs):
    width, n = outs[0].shape
    half = own.shape[0]
    dims = (((0,), (0,)), ((), ()))
    for k, out in enumerate(outs):
        for s in spans(n):
            cols = slice(k * width, (k + 1) * width)
            term = lax.dot_general(tokens[:half, cols], own[:, s], dims, preferred_element_type=F32)
            term += lax.dot_general(tokens[half:, cols], other[:, s], dims, preferred_element_type=F32)
            out[:, s] = term.astype(BF16)


def after(x, *others):
    return lax.optimization_barrier((x, *others))[0]


def per_device(activations, gate_weight, up_weight, hidden_grad):
    index = lax.axis_index("dp")
    core, y, z_bit = index & 1, (index >> 1) & 1, (index >> 2) & 1
    y0, z0 = y == 0, z_bit == 0
    place = jnp.stack([z_bit * 2 + y, core]).astype(jnp.int32)
    rows, width = activations.shape
    half = gate_weight.shape[1] // 2
    block = hidden_grad.shape[0]
    count = 16 * block
    flops = 2 * count * 4 * width * half

    def pick(cond, a, b):
        return jnp.where(cond, a, b)

    def by_member(parts):
        a = [pick(y0, parts[i], parts[i ^ 1]) for i in range(4)]
        return [pick(z0, a[i], a[i ^ 2]) for i in range(4)]

    def pair(mine, other):
        return pick(y0, mine, other), pick(y0, other, mine)

    pieces = by_member(
        [gate_weight[:, :half], gate_weight[:, half:], up_weight[:, :half], up_weight[:, half:]]
    )
    weights = [lax.ppermute(pieces[k], "dp", QUAD_SWAP[k]) for k in (1, 2, 3)]
    mark = pl.pallas_call(
        arrived,
        out_shape=struct((8, 128), F32),
        in_specs=[pl.BlockSpec(memory_space=pl.ANY)] * 3,
        out_specs=VMEM,
        compiler_params=PARAMS,
        cost_estimate=pl.CostEstimate(flops=MARK_FLOPS, bytes_accessed=4096, transcendentals=0),
    )(*weights)
    weights = [pieces[0], *weights]

    raw = lax.all_to_all(
        jnp.broadcast_to(activations[None], (16, rows, width)), ("dp", "tensor"), 0, 0,
        axis_index_groups=QUAD_YHI_GROUPS,
    )
    raw = lax.all_to_all(
        jnp.broadcast_to(raw[None], (4, 16, rows, width)), "tensor", 0, 0, axis_index_groups=X_GROUPS
    )
    raw = raw.reshape(4, 4, 4, 2, block, width)

    tokens, sent = call(
        arrange_and_send, 6, [struct((2 * count, 4 * width)), struct((count, half), F32)], flops
    )(place, mark, raw, *weights)
    got = lax.ppermute(sent, "dp", CORE_SWAP)
    kept = call(keep_sums, 5, struct((count, half), F32), flops)(place, tokens, *weights)
    part = (kept + got).astype(BF16)
    part = lax.all_to_all(part.reshape(8, 2 * block, half), "dp", 0, 0, axis_index_groups=Z_GROUPS)
    gate_pre = jnp.sum(part[0::2].astype(F32), 0)
    up_pre = jnp.sum(part[1::2].astype(F32), 0)

    lo, hi = hidden_grad[:, :half], hidden_grad[:, half:]
    mine, other = pair(lo, hi)
    grad = jnp.concatenate(pair(mine, lax.ppermute(other, "dp", Y_SWAP)), 0).astype(F32)

    sig = jax.nn.sigmoid(gate_pre)
    hidden = (gate_pre * sig * up_pre).astype(BF16)
    gate_back = (grad * up_pre * sig * (1.0 + gate_pre * (1.0 - sig))).astype(BF16)
    up_back = (grad * gate_pre * sig).astype(BF16)

    own = lax.all_to_all(
        jnp.broadcast_to(jnp.stack([gate_back, up_back])[None], (4, 2, 2 * block, half)).reshape(
            8, 2 * block, half
        ),
        "dp", 0, 0, axis_index_groups=Z_GROUPS,
    ).reshape(count, half)
    mine, other = pair(hidden[:block], hidden[block:])
    other = lax.ppermute(other, "dp", Y_SWAP)
    own = after(own, other)
    hidden = jnp.concatenate(pair(mine, other), 1)
    other = lax.ppermute(own, "dp", CORE_SWAP)

    total = call(input_parts, 6, struct((4, 4, 4, 2, block, width)), 2 * flops)(
        place, own, other, *weights
    )
    total = lax.all_to_all(
        total.reshape(4, 16, rows, width), "tensor", 0, 0, axis_index_groups=X_GROUPS
    )
    total = jnp.sum(total.astype(F32), 0).astype(BF16)

    grads = call(weight_parts, 3, [struct((width, half))] * 4, 2 * flops)(place, tokens, own, other)
    grads = [grads[0]] + [lax.ppermute(grads[k], "dp", QUAD_SWAP[k]) for k in (1, 2, 3)]

    total = after(total, grads[1])
    total = lax.all_to_all(total, ("dp", "tensor"), 0, 0, axis_index_groups=QUAD_YHI_GROUPS)
    input_grad = jnp.sum(total.astype(F32), 0).astype(BF16)

    grads = by_member(grads)
    gate_grad = jnp.concatenate(grads[:2], 1)
    up_grad = jnp.concatenate(grads[2:], 1)
    return (hidden, input_grad, gate_grad, up_grad)


def solution(mesh):
    placed = (P("tensor", "dp"), P("dp", "tensor"), P("dp", "tensor"), P("dp", "tensor"))
    return jax.shard_map(
        per_device,
        mesh=mesh,
        in_specs=placed,
        out_specs=(P("dp", "tensor"), P("tensor", "dp"), P("dp", "tensor"), P("dp", "tensor")),
        check_vma=False,
    )
```

```python
import jax
import jax.numpy as jnp
from jax import lax
from jax.experimental import pallas as pl
from jax.experimental.pallas import tpu as pltpu
from jax.sharding import PartitionSpec as P

F32, BF16 = jnp.float32, jnp.bfloat16

CORE_SWAP = [(i, i ^ 1) for i in range(32)]
Y_SWAP = [(i, i ^ 2) for i in range(32)]
QUAD_SWAP = [None, Y_SWAP, [(i, i ^ 4) for i in range(32)], [(i, i ^ 6) for i in range(32)]]
Z_GROUPS = [[z * 4 + r for z in range(8)] for r in range(4)]
X_GROUPS = [[4 * h + x for x in range(4)] for h in range(4)]
QUAD_YHI_GROUPS = [
    [((2 * q + b) * 4 + 2 * y + c) * 16 + 4 * h + x for b in range(2) for y in range(2) for h in range(4)]
    for q in range(4) for c in range(2) for x in range(4)
]

PARAMS = pltpu.CompilerParams(vmem_limit_bytes=32 * 1024 * 1024)
MARK_FLOPS = 30_000_000_000
VMEM = pl.BlockSpec(memory_space=pltpu.VMEM)
SMEM = pl.BlockSpec(memory_space=pltpu.SMEM)


def struct(shape, dtype=BF16):
    return jax.ShapeDtypeStruct(shape, dtype)


def call(kernel, n_in, out_shape, flops, first=SMEM):
    many = isinstance(out_shape, list)
    return pl.pallas_call(
        kernel,
        out_shape=out_shape,
        in_specs=[first] + [VMEM] * n_in,
        out_specs=[VMEM] * len(out_shape) if many else VMEM,
        compiler_params=PARAMS,
        cost_estimate=pl.CostEstimate(flops=flops, bytes_accessed=4 << 20, transcendentals=0),
    )


def spans(n, step=256):
    return [slice(i, min(i + step, n)) for i in range(0, n, step)]


def arrived(*refs):
    out = refs[-1]
    out[...] = jnp.zeros_like(out)


def arrange_and_send(place, mark, raw, w0, w1, w2, w3, tokens, sent):
    width = raw.shape[-1]
    half, block = tokens.shape[0] // 2, raw.shape[-2]
    for part in range(2):
        core = place[1] ^ part
        for k in range(4):
            member = place[0] ^ k
            for h in range(4):
                for x in range(4):
                    row = part * half + (h * 4 + x) * block
                    tokens[row : row + block, k * width : (k + 1) * width] = raw[x, member, h, core]
    for s in spans(sent.shape[1]):
        total = None
        for k, w in enumerate((w0, w1, w2, w3)):
            term = jnp.dot(
                tokens[half:, k * width : (k + 1) * width], w[:, s], preferred_element_type=F32
            )
            total = term if total is None else total + term
        sent[:, s] = total.astype(BF16)


def keep_sums(place, tokens, w0, w1, w2, w3, out):
    width = w0.shape[0]
    half = out.shape[0]
    for s in spans(out.shape[1]):
        total = None
        for k, w in enumerate((w0, w1, w2, w3)):
            term = jnp.dot(
                tokens[:half, k * width : (k + 1) * width], w[:, s], preferred_element_type=F32
            )
            total = term if total is None else total + term
        out[:, s] = total


def input_parts(place, own, other, w0, w1, w2, w3, out):
    block = out.shape[-2]
    for part, back in enumerate((own, other)):
        core = place[1] ^ part
        for k, w in enumerate((w0, w1, w2, w3)):
            member = place[0] ^ k
            term = lax.dot_general(
                back[...], w[...], (((1,), (1,)), ((), ())), preferred_element_type=F32
            ).astype(BF16)
            for h in range(4):
                for x in range(4):
                    row = (h * 4 + x) * block
                    out[x, member, h, core] = term[row : row + block]


def weight_parts(place, tokens, own, other, *outs):
    width, n = outs[0].shape
    half = own.shape[0]
    dims = (((0,), (0,)), ((), ()))
    for k, out in enumerate(outs):
        for s in spans(n):
            cols = slice(k * width, (k + 1) * width)
            term = lax.dot_general(tokens[:half, cols], own[:, s], dims, preferred_element_type=F32)
            term += lax.dot_general(tokens[half:, cols], other[:, s], dims, preferred_element_type=F32)
            out[:, s] = term.astype(BF16)


def sum_first(x, out):
    terms = [x[i].astype(F32) for i in range(x.shape[0])]
    out[...] = ((terms[0] + terms[1]) + (terms[2] + terms[3])).astype(BF16)


def after(x, *others):
    return lax.optimization_barrier((x, *others))[0]


def per_device(activations, gate_weight, up_weight, hidden_grad):
    index = lax.axis_index("dp")
    core, y, z_bit = index & 1, (index >> 1) & 1, (index >> 2) & 1
    y0, z0 = y == 0, z_bit == 0
    place = jnp.stack([z_bit * 2 + y, core]).astype(jnp.int32)
    rows, width = activations.shape
    half = gate_weight.shape[1] // 2
    block = hidden_grad.shape[0]
    count = 16 * block
    flops = 2 * count * 4 * width * half

    def pick(cond, a, b):
        return jnp.where(cond, a, b)

    def by_member(parts):
        a = [pick(y0, parts[i], parts[i ^ 1]) for i in range(4)]
        return [pick(z0, a[i], a[i ^ 2]) for i in range(4)]

    def pair(mine, other):
        return pick(y0, mine, other), pick(y0, other, mine)

    def pieces(gate, up):
        return by_member([gate[:, :half], gate[:, half:], up[:, :half], up[:, half:]])

    sends = pieces(gate_weight, up_weight)
    weights = [lax.ppermute(sends[k], "dp", QUAD_SWAP[k]) for k in (1, 2, 3)]
    mark = pl.pallas_call(
        arrived,
        out_shape=struct((8, 128), F32),
        in_specs=[pl.BlockSpec(memory_space=pl.ANY)] * 2,
        out_specs=VMEM,
        compiler_params=PARAMS,
        cost_estimate=pl.CostEstimate(flops=MARK_FLOPS, bytes_accessed=4096, transcendentals=0),
    )(*weights[:2])

    raw = lax.all_to_all(
        jnp.broadcast_to(activations[None], (16, rows, width)), ("dp", "tensor"), 0, 0,
        axis_index_groups=QUAD_YHI_GROUPS,
    )
    raw, gate, up = lax.optimization_barrier((raw, gate_weight, up_weight))
    weights = [pieces(gate, up)[0], *weights]
    raw = lax.all_to_all(
        jnp.broadcast_to(raw[None], (4, 16, rows, width)), "tensor", 0, 0, axis_index_groups=X_GROUPS
    )
    raw = raw.reshape(4, 4, 4, 2, block, width)

    tokens, sent = call(
        arrange_and_send, 6, [struct((2 * count, 4 * width)), struct((count, half))], flops
    )(place, mark, raw, *weights)
    got = lax.ppermute(sent, "dp", CORE_SWAP)
    kept = call(keep_sums, 5, struct((count, half), F32), flops)(place, tokens, *weights)
    part = (kept + got.astype(F32)).astype(BF16)
    part = lax.all_to_all(part.reshape(8, 2 * block, half), "dp", 0, 0, axis_index_groups=Z_GROUPS)
    gate_pre = jnp.sum(part[0::2].astype(F32), 0)
    up_pre = jnp.sum(part[1::2].astype(F32), 0)

    lo, hi = hidden_grad[:, :half], hidden_grad[:, half:]
    mine, other = pair(lo, hi)
    grad = jnp.concatenate(pair(mine, lax.ppermute(other, "dp", Y_SWAP)), 0).astype(F32)

    sig = jax.nn.sigmoid(gate_pre)
    hidden = (gate_pre * sig * up_pre).astype(BF16)
    gate_back = (grad * up_pre * sig * (1.0 + gate_pre * (1.0 - sig))).astype(BF16)
    up_back = (grad * gate_pre * sig).astype(BF16)

    own = lax.all_to_all(
        jnp.broadcast_to(jnp.stack([gate_back, up_back])[None], (4, 2, 2 * block, half)).reshape(
            8, 2 * block, half
        ),
        "dp", 0, 0, axis_index_groups=Z_GROUPS,
    ).reshape(count, half)
    mine, other = pair(hidden[:block], hidden[block:])
    other = lax.ppermute(other, "dp", Y_SWAP)
    own = after(own, other)
    hidden = jnp.concatenate(pair(mine, other), 1)
    other = lax.ppermute(own, "dp", CORE_SWAP)

    total = call(input_parts, 6, struct((4, 4, 4, 2, block, width)), 2 * flops)(
        place, own, other, *weights
    )
    total = lax.all_to_all(
        total.reshape(4, 16, rows, width), "tensor", 0, 0, axis_index_groups=X_GROUPS
    )
    total = call(sum_first, 0, struct((16, rows, width)), 1 << 20, VMEM)(total)

    grads = call(weight_parts, 3, [struct((width, half))] * 4, 2 * flops)(place, tokens, own, other)
    grads = [grads[0]] + [lax.ppermute(grads[k], "dp", QUAD_SWAP[k]) for k in (1, 2, 3)]

    total = lax.all_to_all(total, ("dp", "tensor"), 0, 0, axis_index_groups=QUAD_YHI_GROUPS)
    input_grad = jnp.sum(total.astype(F32), 0).astype(BF16)

    grads = by_member(grads)
    gate_grad = jnp.concatenate(grads[:2], 1)
    up_grad = jnp.concatenate(grads[2:], 1)
    return (hidden, input_grad, gate_grad, up_grad)


def solution(mesh):
    placed = (P("tensor", "dp"), P("dp", "tensor"), P("dp", "tensor"), P("dp", "tensor"))
    return jax.shard_map(
        per_device,
        mesh=mesh,
        in_specs=placed,
        out_specs=(P("dp", "tensor"), P("tensor", "dp"), P("dp", "tensor"), P("dp", "tensor")),
        check_vma=False,
    )
```

```python
import jax
import jax.numpy as jnp
from jax import lax
from jax.experimental import pallas as pl
from jax.experimental.pallas import tpu as pltpu
from jax.sharding import PartitionSpec as P

F32, BF16 = jnp.float32, jnp.bfloat16

CORE_SWAP = [(i, i ^ 1) for i in range(32)]
Y_SWAP = [(i, i ^ 2) for i in range(32)]
QUAD_SWAP = [None, Y_SWAP, [(i, i ^ 4) for i in range(32)], [(i, i ^ 6) for i in range(32)]]
Z_GROUPS = [[z * 4 + r for z in range(8)] for r in range(4)]
X_GROUPS = [[4 * h + x for x in range(4)] for h in range(4)]
QUAD_YHI_GROUPS = [
    [((2 * q + b) * 4 + 2 * y + c) * 16 + 4 * h + x for b in range(2) for y in range(2) for h in range(4)]
    for q in range(4) for c in range(2) for x in range(4)
]

PARAMS = pltpu.CompilerParams(vmem_limit_bytes=32 * 1024 * 1024)
MARK_FLOPS = 30_000_000_000
VMEM = pl.BlockSpec(memory_space=pltpu.VMEM)
SMEM = pl.BlockSpec(memory_space=pltpu.SMEM)
ANY = pl.BlockSpec(memory_space=pl.ANY)


def struct(shape, dtype=BF16):
    return jax.ShapeDtypeStruct(shape, dtype)


def call(kernel, n_in, out_shape, flops, first=SMEM, last=VMEM, scratch=()):
    many = isinstance(out_shape, list)
    return pl.pallas_call(
        kernel,
        out_shape=out_shape,
        in_specs=[first] + [VMEM] * n_in,
        out_specs=[last] * len(out_shape) if many else last,
        scratch_shapes=scratch,
        compiler_params=PARAMS,
        cost_estimate=pl.CostEstimate(flops=flops, bytes_accessed=4 << 20, transcendentals=0),
    )


def spans(n, step=256):
    return [slice(i, min(i + step, n)) for i in range(0, n, step)]


def arrived(*refs):
    out = refs[-1]
    out[...] = jnp.zeros_like(out)


def arrange_and_send(place, mark, raw, w0, w1, w2, w3, tokens, sent):
    width = raw.shape[-1]
    half, block = tokens.shape[0] // 2, raw.shape[-2]
    for part in range(2):
        core = place[1] ^ part
        for k in range(4):
            member = place[0] ^ k
            for h in range(4):
                for x in range(4):
                    row = part * half + (h * 4 + x) * block
                    tokens[row : row + block, k * width : (k + 1) * width] = raw[x, member, h, core]
    for s in spans(sent.shape[1]):
        total = None
        for k, w in enumerate((w0, w1, w2, w3)):
            term = jnp.dot(
                tokens[half:, k * width : (k + 1) * width], w[:, s], preferred_element_type=F32
            )
            total = term if total is None else total + term
        sent[:, s] = total.astype(BF16)


def keep_sums(place, tokens, w0, w1, w2, w3, out):
    width = w0.shape[0]
    half = out.shape[0]
    for s in spans(out.shape[1]):
        total = None
        for k, w in enumerate((w0, w1, w2, w3)):
            term = jnp.dot(
                tokens[:half, k * width : (k + 1) * width], w[:, s], preferred_element_type=F32
            )
            total = term if total is None else total + term
        out[:, s] = total


def input_parts(place, own, other, w0, w1, w2, w3, out, held, sems):
    block = out.shape[-2]
    copies = []
    for k, w in enumerate((w0, w1, w2, w3)):
        for part, back in enumerate((own, other)):
            core = place[1] ^ part
            term = lax.dot_general(
                back[...], w[...], (((1,), (1,)), ((), ())), preferred_element_type=F32
            ).astype(BF16)
            for h in range(4):
                for x in range(4):
                    row = (h * 4 + x) * block
                    held[k, x, h, core] = term[row : row + block]
        copies.append(pltpu.make_async_copy(held.at[k], out.at[:, place[0] ^ k], sems.at[k]))
        copies[-1].start()
    for copy in copies:
        copy.wait()


def weight_parts(place, tokens, own, other, *refs):
    outs, held, sems = refs[:4], refs[4], refs[5]
    width, n = outs[0].shape
    half = own.shape[0]
    dims = (((0,), (0,)), ((), ()))
    copies = []
    for k in (1, 2, 3, 0):
        for s in spans(n):
            cols = slice(k * width, (k + 1) * width)
            term = lax.dot_general(tokens[:half, cols], own[:, s], dims, preferred_element_type=F32)
            term += lax.dot_general(tokens[half:, cols], other[:, s], dims, preferred_element_type=F32)
            held[k, :, s] = term.astype(BF16)
        copies.append(pltpu.make_async_copy(held.at[k], outs[k], sems.at[k]))
        copies[-1].start()
    for copy in copies:
        copy.wait()


def sum_first(x, out):
    terms = [x[i].astype(F32) for i in range(x.shape[0])]
    out[...] = ((terms[0] + terms[1]) + (terms[2] + terms[3])).astype(BF16)


def after(x, *others):
    return lax.optimization_barrier((x, *others))[0]


def per_device(activations, gate_weight, up_weight, hidden_grad):
    index = lax.axis_index("dp")
    core, y, z_bit = index & 1, (index >> 1) & 1, (index >> 2) & 1
    y0, z0 = y == 0, z_bit == 0
    place = jnp.stack([z_bit * 2 + y, core]).astype(jnp.int32)
    rows, width = activations.shape
    half = gate_weight.shape[1] // 2
    block = hidden_grad.shape[0]
    count = 16 * block
    flops = 2 * count * 4 * width * half

    def pick(cond, a, b):
        return jnp.where(cond, a, b)

    def by_member(parts):
        a = [pick(y0, parts[i], parts[i ^ 1]) for i in range(4)]
        return [pick(z0, a[i], a[i ^ 2]) for i in range(4)]

    def pair(mine, other):
        return pick(y0, mine, other), pick(y0, other, mine)

    def pieces(gate, up):
        return by_member([gate[:, :half], gate[:, half:], up[:, :half], up[:, half:]])

    sends = pieces(gate_weight, up_weight)
    weights = [lax.ppermute(sends[k], "dp", QUAD_SWAP[k]) for k in (1, 2, 3)]
    mark = pl.pallas_call(
        arrived,
        out_shape=struct((8, 128), F32),
        in_specs=[ANY] * 2,
        out_specs=VMEM,
        compiler_params=PARAMS,
        cost_estimate=pl.CostEstimate(flops=MARK_FLOPS, bytes_accessed=4096, transcendentals=0),
    )(*weights[:2])

    raw = lax.all_to_all(
        jnp.broadcast_to(activations[None], (16, rows, width)), ("dp", "tensor"), 0, 0,
        axis_index_groups=QUAD_YHI_GROUPS,
    )
    raw, gate, up = lax.optimization_barrier((raw, gate_weight, up_weight))
    weights = [pieces(gate, up)[0], *weights]
    raw = lax.all_to_all(
        jnp.broadcast_to(raw[None], (4, 16, rows, width)), "tensor", 0, 0, axis_index_groups=X_GROUPS
    )
    raw = raw.reshape(4, 4, 4, 2, block, width)

    tokens, sent = call(
        arrange_and_send, 6, [struct((2 * count, 4 * width)), struct((count, half))], flops
    )(place, mark, raw, *weights)
    got = lax.ppermute(sent, "dp", CORE_SWAP)
    kept = call(keep_sums, 5, struct((count, half), F32), flops)(place, tokens, *weights)
    part = (kept + got.astype(F32)).astype(BF16)
    part = lax.all_to_all(part.reshape(8, 2 * block, half), "dp", 0, 0, axis_index_groups=Z_GROUPS)
    gate_pre = jnp.sum(part[0::2].astype(F32), 0)
    up_pre = jnp.sum(part[1::2].astype(F32), 0)

    lo, hi = hidden_grad[:, :half], hidden_grad[:, half:]
    mine, other = pair(lo, hi)
    grad = jnp.concatenate(pair(mine, lax.ppermute(other, "dp", Y_SWAP)), 0).astype(F32)

    sig = jax.nn.sigmoid(gate_pre)
    hidden = (gate_pre * sig * up_pre).astype(BF16)
    gate_back = (grad * up_pre * sig * (1.0 + gate_pre * (1.0 - sig))).astype(BF16)
    up_back = (grad * gate_pre * sig).astype(BF16)

    own = lax.all_to_all(
        jnp.broadcast_to(jnp.stack([gate_back, up_back])[None], (4, 2, 2 * block, half)).reshape(
            8, 2 * block, half
        ),
        "dp", 0, 0, axis_index_groups=Z_GROUPS,
    ).reshape(count, half)
    mine, other = pair(hidden[:block], hidden[block:])
    other = lax.ppermute(other, "dp", Y_SWAP)
    own = after(own, other)
    hidden = jnp.concatenate(pair(mine, other), 1)
    other = lax.ppermute(own, "dp", CORE_SWAP)

    sems = pltpu.SemaphoreType.DMA((4,))
    scratch = [pltpu.VMEM((4, 4, 4, 2, block, width), BF16), sems]
    total = call(
        input_parts, 6, struct((4, 4, 4, 2, block, width)), 2 * flops, last=ANY, scratch=scratch
    )(place, own, other, *weights)
    total = lax.all_to_all(
        total.reshape(4, 16, rows, width), "tensor", 0, 0, axis_index_groups=X_GROUPS
    )
    total = call(sum_first, 0, struct((16, rows, width)), 1 << 20, VMEM)(total)

    scratch = [pltpu.VMEM((4, width, half), BF16), sems]
    grads = call(
        weight_parts, 3, [struct((width, half))] * 4, 2 * flops, last=ANY, scratch=scratch
    )(place, tokens, own, other)
    grads = [grads[0]] + [lax.ppermute(grads[k], "dp", QUAD_SWAP[k]) for k in (1, 2, 3)]

    total = lax.all_to_all(total, ("dp", "tensor"), 0, 0, axis_index_groups=QUAD_YHI_GROUPS)
    input_grad = jnp.sum(total.astype(F32), 0).astype(BF16)

    grads = by_member(grads)
    gate_grad = jnp.concatenate(grads[:2], 1)
    up_grad = jnp.concatenate(grads[2:], 1)
    return (hidden, input_grad, gate_grad, up_grad)


def solution(mesh):
    placed = (P("tensor", "dp"), P("dp", "tensor"), P("dp", "tensor"), P("dp", "tensor"))
    return jax.shard_map(
        per_device,
        mesh=mesh,
        in_specs=placed,
        out_specs=(P("dp", "tensor"), P("tensor", "dp"), P("dp", "tensor"), P("dp", "tensor")),
        check_vma=False,
    )
```

```python
import jax
import jax.numpy as jnp
from jax import lax
from jax.experimental import pallas as pl
from jax.experimental.pallas import tpu as pltpu
from jax.sharding import PartitionSpec as P

F32, BF16 = jnp.float32, jnp.bfloat16

CORE_SWAP = [(i, i ^ 1) for i in range(32)]
Y_SWAP = [(i, i ^ 2) for i in range(32)]
QUAD_SWAP = [None, Y_SWAP, [(i, i ^ 4) for i in range(32)], [(i, i ^ 6) for i in range(32)]]
Z_GROUPS = [[z * 4 + r for z in range(8)] for r in range(4)]
X_GROUPS = [[4 * h + x for x in range(4)] for h in range(4)]
QUAD_YHI_GROUPS = [
    [((2 * q + b) * 4 + 2 * y + c) * 16 + 4 * h + x for b in range(2) for y in range(2) for h in range(4)]
    for q in range(4) for c in range(2) for x in range(4)
]

PARAMS = pltpu.CompilerParams(vmem_limit_bytes=32 * 1024 * 1024)
MARK_FLOPS = 30_000_000_000
VMEM = pl.BlockSpec(memory_space=pltpu.VMEM)
SMEM = pl.BlockSpec(memory_space=pltpu.SMEM)
ANY = pl.BlockSpec(memory_space=pl.ANY)


def struct(shape, dtype=BF16):
    return jax.ShapeDtypeStruct(shape, dtype)


def call(kernel, n_in, out_shape, flops, first=SMEM, last=VMEM, scratch=()):
    many = isinstance(out_shape, list)
    return pl.pallas_call(
        kernel,
        out_shape=out_shape,
        in_specs=[first] + [VMEM] * n_in,
        out_specs=[last] * len(out_shape) if many else last,
        scratch_shapes=scratch,
        compiler_params=PARAMS,
        cost_estimate=pl.CostEstimate(flops=flops, bytes_accessed=4 << 20, transcendentals=0),
    )


def spans(n, step=256):
    return [slice(i, min(i + step, n)) for i in range(0, n, step)]


def arrived(*refs):
    out = refs[-1]
    out[...] = jnp.zeros_like(out)


def arrange_and_send(place, mark, raw, w0, w1, w2, w3, tokens, sent):
    width = raw.shape[-1]
    half, block = tokens.shape[0] // 2, raw.shape[-2]
    for part in range(2):
        core = place[1] ^ part
        for k in range(4):
            member = place[0] ^ k
            for h in range(4):
                for x in range(4):
                    row = part * half + (h * 4 + x) * block
                    tokens[row : row + block, k * width : (k + 1) * width] = raw[x, member, h, core]
    for s in spans(sent.shape[1]):
        total = None
        for k, w in enumerate((w0, w1, w2, w3)):
            term = jnp.dot(
                tokens[half:, k * width : (k + 1) * width], w[:, s], preferred_element_type=F32
            )
            total = term if total is None else total + term
        sent[:, s] = total


def keep_sums(place, tokens, w0, w1, w2, w3, out):
    width = w0.shape[0]
    half = out.shape[0]
    for s in spans(out.shape[1]):
        total = None
        for k, w in enumerate((w0, w1, w2, w3)):
            term = jnp.dot(
                tokens[:half, k * width : (k + 1) * width], w[:, s], preferred_element_type=F32
            )
            total = term if total is None else total + term
        out[:, s] = total


def input_parts(place, own, other, w0, w1, w2, w3, out, held, sems):
    block = out.shape[-2]
    copies = []
    for k, w in enumerate((w0, w1, w2, w3)):
        for part, back in enumerate((own, other)):
            core = place[1] ^ part
            term = lax.dot_general(
                back[...], w[...], (((1,), (1,)), ((), ())), preferred_element_type=F32
            ).astype(BF16)
            for h in range(4):
                for x in range(4):
                    row = (h * 4 + x) * block
                    held[k, x, h, core] = term[row : row + block]
        copies.append(pltpu.make_async_copy(held.at[k], out.at[:, place[0] ^ k], sems.at[k]))
        copies[-1].start()
    for copy in copies:
        copy.wait()


def weight_parts(place, tokens, own, other, *refs):
    outs, held, sems = refs[:4], refs[4], refs[5]
    width, n = outs[0].shape
    half = own.shape[0]
    dims = (((0,), (0,)), ((), ()))
    copies = []
    for k in (1, 2, 3, 0):
        for s in spans(n):
            cols = slice(k * width, (k + 1) * width)
            term = lax.dot_general(tokens[:half, cols], own[:, s], dims, preferred_element_type=F32)
            term += lax.dot_general(tokens[half:, cols], other[:, s], dims, preferred_element_type=F32)
            held[k, :, s] = term.astype(BF16)
        copies.append(pltpu.make_async_copy(held.at[k], outs[k], sems.at[k]))
        copies[-1].start()
    for copy in copies:
        copy.wait()


def sum_first(x, out):
    terms = [x[i].astype(F32) for i in range(x.shape[0])]
    out[...] = ((terms[0] + terms[1]) + (terms[2] + terms[3])).astype(BF16)


def after(x, *others):
    return lax.optimization_barrier((x, *others))[0]


def per_device(activations, gate_weight, up_weight, hidden_grad):
    index = lax.axis_index("dp")
    core, y, z_bit = index & 1, (index >> 1) & 1, (index >> 2) & 1
    y0, z0 = y == 0, z_bit == 0
    place = jnp.stack([z_bit * 2 + y, core]).astype(jnp.int32)
    rows, width = activations.shape
    half = gate_weight.shape[1] // 2
    block = hidden_grad.shape[0]
    count = 16 * block
    flops = 2 * count * 4 * width * half

    def pick(cond, a, b):
        return jnp.where(cond, a, b)

    def by_member(parts):
        a = [pick(y0, parts[i], parts[i ^ 1]) for i in range(4)]
        return [pick(z0, a[i], a[i ^ 2]) for i in range(4)]

    def pair(mine, other):
        return pick(y0, mine, other), pick(y0, other, mine)

    def pieces(gate, up):
        return by_member([gate[:, :half], gate[:, half:], up[:, :half], up[:, half:]])

    sends = pieces(gate_weight, up_weight)
    weights = [lax.ppermute(sends[k], "dp", QUAD_SWAP[k]) for k in (1, 2, 3)]
    mark = pl.pallas_call(
        arrived,
        out_shape=struct((8, 128), F32),
        in_specs=[ANY] * 2,
        out_specs=VMEM,
        compiler_params=PARAMS,
        cost_estimate=pl.CostEstimate(flops=MARK_FLOPS, bytes_accessed=4096, transcendentals=0),
    )(*weights[:2])

    raw = lax.all_to_all(
        jnp.broadcast_to(activations[None], (16, rows, width)), ("dp", "tensor"), 0, 0,
        axis_index_groups=QUAD_YHI_GROUPS,
    )
    raw, gate, up = lax.optimization_barrier((raw, gate_weight, up_weight))
    weights = [pieces(gate, up)[0], *weights]
    raw = lax.all_to_all(
        jnp.broadcast_to(raw[None], (4, 16, rows, width)), "tensor", 0, 0, axis_index_groups=X_GROUPS
    )
    raw = raw.reshape(4, 4, 4, 2, block, width)

    tokens, sent = call(
        arrange_and_send, 6, [struct((2 * count, 4 * width)), struct((count, half), F32)], flops
    )(place, mark, raw, *weights)
    got = lax.ppermute(sent, "dp", CORE_SWAP)
    kept = call(keep_sums, 5, struct((count, half), F32), flops)(place, tokens, *weights)
    part = (kept + got).astype(BF16)
    part = lax.all_to_all(part.reshape(8, 2 * block, half), "dp", 0, 0, axis_index_groups=Z_GROUPS)
    gate_pre = jnp.sum(part[0::2].astype(F32), 0)
    up_pre = jnp.sum(part[1::2].astype(F32), 0)

    lo, hi = hidden_grad[:, :half], hidden_grad[:, half:]
    mine, other = pair(lo, hi)
    grad = jnp.concatenate(pair(mine, lax.ppermute(other, "dp", Y_SWAP)), 0).astype(F32)

    sig = jax.nn.sigmoid(gate_pre)
    hidden = (gate_pre * sig * up_pre).astype(BF16)
    gate_back = (grad * up_pre * sig * (1.0 + gate_pre * (1.0 - sig))).astype(BF16)
    up_back = (grad * gate_pre * sig).astype(BF16)

    own = lax.all_to_all(
        jnp.broadcast_to(jnp.stack([gate_back, up_back])[None], (4, 2, 2 * block, half)).reshape(
            8, 2 * block, half
        ),
        "dp", 0, 0, axis_index_groups=Z_GROUPS,
    ).reshape(count, half)
    mine, other = pair(hidden[:block], hidden[block:])
    other = lax.ppermute(other, "dp", Y_SWAP)
    own = after(own, other)
    hidden = jnp.concatenate(pair(mine, other), 1)
    other = lax.ppermute(own, "dp", CORE_SWAP)

    sems = pltpu.SemaphoreType.DMA((4,))
    scratch = [pltpu.VMEM((4, 4, 4, 2, block, width), BF16), sems]
    total = call(
        input_parts, 6, struct((4, 4, 4, 2, block, width)), 2 * flops, last=ANY, scratch=scratch
    )(place, own, other, *weights)
    total = lax.all_to_all(
        total.reshape(4, 16, rows, width), "tensor", 0, 0, axis_index_groups=X_GROUPS
    )
    total = call(sum_first, 0, struct((16, rows, width)), 1 << 20, VMEM)(total)

    scratch = [pltpu.VMEM((4, width, half), BF16), sems]
    grads = call(
        weight_parts, 3, [struct((width, half))] * 4, 2 * flops, last=ANY, scratch=scratch
    )(place, tokens, own, other)
    grads = [grads[0]] + [lax.ppermute(grads[k], "dp", QUAD_SWAP[k]) for k in (1, 2, 3)]

    total = lax.all_to_all(total, ("dp", "tensor"), 0, 0, axis_index_groups=QUAD_YHI_GROUPS)
    input_grad = jnp.sum(total.astype(F32), 0).astype(BF16)

    grads = by_member(grads)
    gate_grad = jnp.concatenate(grads[:2], 1)
    up_grad = jnp.concatenate(grads[2:], 1)
    return (hidden, input_grad, gate_grad, up_grad)


def solution(mesh):
    placed = (P("tensor", "dp"), P("dp", "tensor"), P("dp", "tensor"), P("dp", "tensor"))
    return jax.shard_map(
        per_device,
        mesh=mesh,
        in_specs=placed,
        out_specs=(P("dp", "tensor"), P("tensor", "dp"), P("dp", "tensor"), P("dp", "tensor")),
        check_vma=False,
    )
```
